32 devices in a mesh: shard: 2 (over core), heads: 4 (over y, x), tensor: 4 (over z).
Axes of the slice: x: 2, y: 2, z: 4, core: 2. Of those that a mesh axis runs over, the one named last changes fastest.
Arguments:
- tokens: bfloat16 [8, 2048, 768], P(('shard', 'tensor'), 'heads'), may hold values from -6 to 6
- ln1_gain: bfloat16 [768], P('shard'), may hold values from 0.5 to 1.5
- ln1_bias: bfloat16 [768], P('shard'), may hold values from -2 to 2
- w_qkv: bfloat16 [768, 2304], P('shard'), may hold values from -0.21875 to 0.21875
- bias_qv: bfloat16 [2, 768], P(None, 'shard'), may hold values from -2 to 2
- w_out: bfloat16 [768, 768], P('shard'), may hold values from -0.875 to 0.875
- bias_out: bfloat16 [768], P('shard'), may hold values from -2 to 2
- ln2_gain: bfloat16 [768], P('shard'), may hold values from 0.5 to 1.5
- ln2_bias: bfloat16 [768], P('shard'), may hold values from -2 to 2
- w_in: bfloat16 [3072, 768], P(('shard', 'tensor')), may hold values from -0.21875 to 0.21875
- bias_in: bfloat16 [3072], P(('shard', 'tensor')), may hold values from -2 to 2
- w_back: bfloat16 [3072, 768], P(('shard', 'tensor')), may hold values from -0.109375 to 0.109375
- bias_back: bfloat16 [768], P('shard'), may hold values from -2 to 2
- seq_lengths: int32 [8, 4], P(('shard', 'tensor')), may hold values from 1 to 1024, 2048 in all within a row
- cotangent: bfloat16 [8, 2048, 768], P(('shard', 'tensor'), 'heads'), may hold values from -6 to 6
Outputs:
- output: bfloat16 [8, 2048, 768], P(('shard', 'tensor'), 'heads')
- input_grad: bfloat16 [8, 2048, 768], P(('shard', 'tensor'), 'heads')
- grad_ln1_gain: float32 [768], P('shard')
- grad_ln1_bias: float32 [768], P('shard')
- grad_w_qkv: float32 [768, 2304], P('shard')
- grad_bias_qv: float32 [2, 768], P(None, 'shard')
- grad_w_out: float32 [768, 768], P('shard')
- grad_bias_out: float32 [768], P('shard')
- grad_ln2_gain: float32 [768], P('shard')
- grad_ln2_bias: float32 [768], P('shard')
- grad_w_in: float32 [3072, 768], P(('shard', 'tensor'))
- grad_bias_in: float32 [3072], P(('shard', 'tensor'))
- grad_w_back: float32 [3072, 768], P(('shard', 'tensor'))
- grad_bias_back: float32 [768], P('shard')
The draws below stay inside these ranges and needn't reach their ends.
Inputs may be any that keep to these rules, and one draw needn't show every extreme that they name: `seq_lengths`: each row sums to 2048, and its largest length is exactly 1024.
All inputs are finite; a program needn't handle non-finite values.
Results may differ from the reference program's by a relative error of at most 0.012.
Values may be sent and summed in bfloat16 or wider, within the bound.
A program may use at most 128 MiB of HBM per device.

```python
import math
from functools import partial
import jax
import jax.numpy as jnp
import numpy as np
from jax import lax

D = 768
HEADS = 12
HEAD_DIM = 64
FF = 3072
NSEQ = 4
GROUP_TOK = 2048
LONGEST = 1024
GROUPS = 8


def block_levels(key, shape, cuts, low, largest):
    level, own = 1.0, jax.random.fold_in(key, 6)
    for axis_at, blocks in cuts:
        steps = jnp.exp(jax.random.uniform(jax.random.fold_in(own, axis_at), (blocks,), jnp.float32, low / len(cuts), largest / len(cuts)))
        level = level * jnp.repeat(steps, shape[axis_at] // blocks).reshape([-1 if axis == axis_at else 1 for axis in range(len(shape))])
    return level


def split_up(number_of, total, reach, lean):
    weights = [(1 << 20) // math.isqrt(standing ** lean) + 1 for standing in range(2, number_of + 1)]
    surplus, counts = total - reach - (number_of - 1), [1] * (number_of - 1)
    while surplus > 0:
        free = [i for i in range(number_of - 1) if counts[i] < reach]
        whole, budget = sum([weights[i] for i in free]), surplus
        for i in free:
            addition = min(reach - counts[i], max(1, budget * weights[i] // whole), surplus)
            counts[i] = counts[i] + addition
            surplus = surplus - addition
    return np.array([reach] + counts)


def uneven(stream_key, number_of, total, reach, skew):
    if number_of == 2:
        one = jax.random.randint(stream_key, (), max(1, total - reach), min(reach, total - 1) + 1)
        return jnp.stack([one, total - one])
    tallies = jnp.asarray(split_up(number_of, total, reach, skew), jnp.int32)
    pairs = (number_of - 1) // 2
    giver, taker = tallies[1:1 + 2 * pairs:2], tallies[2:2 + 2 * pairs:2]
    room = jnp.minimum(giver - 1, reach - taker)
    moved = jax.random.randint(jax.random.fold_in(stream_key, 1), (pairs,), 0, 1 << 20) % (room + 1)
    tallies = tallies.at[1:1 + 2 * pairs:2].set(giver - moved).at[2:2 + 2 * pairs:2].set(taker + moved)
    return tallies[jax.random.permutation(jax.random.fold_in(stream_key, 2), number_of)]


def scatter_about(own_key, shape, scale, most, shards=(), kind=jnp.bfloat16):
    values = scale * jax.random.normal(own_key, shape, jnp.float32)
    if shards:
        values = values * block_levels(own_key, shape, shards, -0.22, 0.18)
    return jnp.clip(values, -most, most).astype(kind)


def setup_inputs(seed: int = 0) -> dict:
    seeds = jax.random.split(jax.random.key(seed), 16)
    return {
        "tokens": scatter_about(seeds[0], (GROUPS, GROUP_TOK, D), 1.0, 6.0, ((0, 8), (1, 4))),
        "ln1_gain": jnp.clip(1.0 + 0.1 * jax.random.normal(seeds[1], (D,), jnp.float32), 0.5, 1.5).astype(jnp.bfloat16),
        "ln1_bias": scatter_about(seeds[2], (D,), 0.3, 2.0, ((0, 2),)),
        "w_qkv": scatter_about(seeds[3], (D, 3 * D), D ** -0.5, 0.21875, ((0, 2),)),
        "bias_qv": scatter_about(seeds[4], (2, D), 0.3, 2.0, ((1, 2),)),
        "w_out": scatter_about(seeds[5], (D, D), (D // 16) ** -0.5, 0.875, ((0, 2),)),
        "bias_out": scatter_about(seeds[6], (D,), 0.3, 2.0, ((0, 2),)),
        "ln2_gain": jnp.clip(1.0 + 0.1 * jax.random.normal(seeds[7], (D,), jnp.float32), 0.5, 1.5).astype(jnp.bfloat16),
        "ln2_bias": scatter_about(seeds[8], (D,), 0.3, 2.0, ((0, 2),)),
        "w_in": scatter_about(seeds[9], (FF, D), D ** -0.5, 0.21875, ((0, 8),)),
        "bias_in": scatter_about(seeds[10], (FF,), 0.3, 2.0, ((0, 8),)),
        "w_back": scatter_about(seeds[11], (FF, D), FF ** -0.5, 0.109375, ((0, 8),)),
        "bias_back": scatter_about(seeds[12], (D,), 0.3, 2.0, ((0, 2),)),
        "seq_lengths": jax.vmap(lambda own: uneven(own, NSEQ, GROUP_TOK, LONGEST, 2))(jax.random.split(seeds[13], GROUPS)).reshape((GROUPS, NSEQ)).astype(jnp.int32),
        "cotangent": scatter_about(seeds[14], (GROUPS, GROUP_TOK, D), 1.0, 6.0, ((0, 8), (1, 4))),
    }


EPSILON = 1e-05
NEGATIVE = -1e+30
HIGH = lax.Precision.HIGHEST

@jax.custom_vjp
def low(v):
    return lax.optimization_barrier(v.astype(jnp.bfloat16)).astype(jnp.float32)

@jax.custom_vjp
def low_back(v):
    return v

def low_keep(v):
    return (low(v), None)

def low_pass(kept, grad):
    return (grad,)

def back_keep(v):
    return (v, None)

def back_low(kept, grad):
    return (low(grad),)
low.defvjp(low_keep, low_pass)
low_back.defvjp(back_keep, back_low)

def layer_norm(values, gain, shift):
    center = lax.optimization_barrier(jnp.mean(values, axis=-1, keepdims=True))
    offset = values - center
    spread = lax.optimization_barrier(jnp.mean(offset * offset, axis=-1, keepdims=True))
    return offset * lax.rsqrt(spread + EPSILON) * gain + shift

def segment_ids(lengths, count):
    ends = jnp.cumsum(lengths).astype(jnp.int32)
    positions = jnp.arange(count, dtype=jnp.int32)
    return lax.optimization_barrier(jnp.sum((ends[None, :] <= positions[:, None]).astype(jnp.int32), axis=1)).astype(jnp.int32)

def layer_group(inputs, segment, params):
    gain_one, shift_one, full_qkv, qv_bias, full_out, out_bias, gain_two, shift_two, full_in, in_bias, full_back, back_bias = params
    attn_in = low(layer_norm(inputs, gain_one, shift_one))
    qkv_bias = jnp.concatenate([qv_bias[0], jnp.zeros((D,), jnp.float32), qv_bias[1]])
    projected = low_back(low(jnp.dot(attn_in, full_qkv, precision=HIGH) + qkv_bias))
    queries = projected[:, :D].reshape(GROUP_TOK, HEADS, HEAD_DIM)
    keys = projected[:, D:2 * D].reshape(GROUP_TOK, HEADS, HEAD_DIM)
    values = projected[:, 2 * D:].reshape(GROUP_TOK, HEADS, HEAD_DIM)
    block = min(512, GROUP_TOK)
    scale = HEAD_DIM ** (-0.5)
    positions = jnp.arange(GROUP_TOK, dtype=jnp.int32)

    def one_block(number):
        start = (number * block).astype(jnp.int32)
        query_block = lax.dynamic_slice_in_dim(queries, start, block, 0)
        scores = low_back(jnp.einsum('qhd,khd->hqk', query_block, keys, precision=HIGH) * scale)
        seg_block = lax.dynamic_slice_in_dim(segment, start, block, 0)
        pos_block = start + jnp.arange(block, dtype=jnp.int32)
        allowed = (seg_block[:, None] == segment[None, :]) & (positions[None, :] <= pos_block[:, None])
        probs = jax.nn.softmax(jnp.where(allowed[None], scores, NEGATIVE), axis=-1)
        return jnp.einsum('hqk,khd->qhd', low(probs), values, precision=HIGH)
    attended = lax.map(jax.checkpoint(one_block), jnp.arange(GROUP_TOK // block, dtype=jnp.int32))
    attended = low_back(low(attended.reshape(GROUP_TOK, D)))
    hidden_res = inputs + low_back(jnp.dot(attended, full_out, precision=HIGH) + out_bias)
    mlp_in = low(layer_norm(hidden_res, gain_two, shift_two))
    pre_act = low_back(lax.dot_general(mlp_in, full_in, (((1,), (1,)), ((), ())), precision=HIGH) + in_bias)
    act = low(jax.nn.gelu(pre_act, approximate=True))
    return hidden_res + low_back(jnp.dot(act, full_back, precision=HIGH) + back_bias)

def reference(tokens, ln1_gain, ln1_bias, w_qkv, bias_qv, w_out, bias_out, ln2_gain, ln2_bias, w_in, bias_in, w_back, bias_back, seq_lengths, cotangent):
    segments = jax.vmap(partial(segment_ids, count=GROUP_TOK))(seq_lengths)
    params = (ln1_gain.astype(jnp.float32), ln1_bias.astype(jnp.float32), w_qkv.astype(jnp.float32), bias_qv.astype(jnp.float32), w_out.astype(jnp.float32), bias_out.astype(jnp.float32), ln2_gain.astype(jnp.float32), ln2_bias.astype(jnp.float32), w_in.astype(jnp.float32), bias_in.astype(jnp.float32), w_back.astype(jnp.float32), bias_back.astype(jnp.float32))
    checked = jax.checkpoint(layer_group)

    def forward(inputs, weights):

        def one_group(carry, item):
            return (carry, checked(item[0], item[1], weights))
        unused, results = lax.scan(one_group, None, (inputs, segments))
        return results
    result, pullback = jax.vjp(forward, tokens.astype(jnp.float32), params)
    grad_inputs, grads = pullback(cotangent.astype(jnp.float32))
    return (result.astype(jnp.bfloat16), grad_inputs.astype(jnp.bfloat16), grads[0], grads[1], grads[2], grads[3], grads[4], grads[5], grads[6], grads[7], grads[8], grads[9], grads[10], grads[11])
```

```python
import math

import jax
import jax.numpy as jnp
from jax import lax
from jax.experimental import pallas as pl
from jax.experimental.pallas import tpu as pltpu
from jax.sharding import PartitionSpec as P

HEAD_DIM = 64
BLOCK = 256
LONGEST = 1024
VMEM_BYTES = 48 * 1024 * 1024


EPSILON = 1e-05
NEGATIVE = -1e30


def layer_norm(values, gain, shift):
    center = jnp.mean(values, axis=-1, keepdims=True)
    offset = values - center
    spread = jnp.mean(offset * offset, axis=-1, keepdims=True)
    return offset * lax.rsqrt(spread + EPSILON) * gain + shift


def gelu_tanh(values):
    return jax.nn.gelu(values, approximate=True)


def contract_last(left, right):
    return lax.dot_general(
        left, right, (((1,), (1,)), ((), ())), preferred_element_type=jnp.float32
    )


def contract_first(left, right):
    return lax.dot_general(
        left, right, (((0,), (0,)), ((), ())), preferred_element_type=jnp.float32
    )


def sequence_starts(lengths, count):
    ends = jnp.cumsum(lengths)
    positions = jnp.arange(count, dtype=jnp.int32)
    past = ends[None, :] <= positions[:, None]
    return jnp.max(jnp.where(past, ends[None, :], 0), axis=1)


def window(number):
    start = number * BLOCK
    return start, max(0, start - LONGEST)


def block_scores(query, key_ref, first_ref, start, low):
    first = first_ref[start : start + BLOCK, 0:1]
    rows = lax.broadcasted_iota(jnp.int32, (BLOCK, BLOCK), 0)
    cols = lax.broadcasted_iota(jnp.int32, (BLOCK, BLOCK), 1)
    own = contract_last(query, key_ref[0, start : start + BLOCK, :])
    own = jnp.where((cols <= rows) & (cols >= first - start), own, NEGATIVE)
    if low == start:
        return own, None
    before = contract_last(query, key_ref[0, low:start, :])
    cols = lax.broadcasted_iota(jnp.int32, (BLOCK, start - low), 1)
    before = jnp.where(cols >= first - low, before, NEGATIVE)
    return own, before


def attend_kernel(first_ref, q_ref, k_ref, v_ref, out_ref, log_ref):
    group_len = q_ref.shape[1]
    for number in range(group_len // BLOCK):
        start, low = window(number)
        stop = start + BLOCK
        query = q_ref[0, start:stop, :]
        own, before = block_scores(query, k_ref, first_ref, start, low)
        largest = jnp.max(own, axis=1, keepdims=True)
        if before is not None:
            largest = jnp.maximum(largest, jnp.max(before, axis=1, keepdims=True))
        own = jnp.exp(own - largest)
        total = jnp.sum(own, axis=1, keepdims=True)
        if before is not None:
            before = jnp.exp(before - largest)
            total = total + jnp.sum(before, axis=1, keepdims=True)
        inverse = 1.0 / total
        result = jnp.dot(
            (own * inverse).astype(jnp.bfloat16),
            v_ref[0, start:stop, :],
            preferred_element_type=jnp.float32,
        )
        if before is not None:
            result = result + jnp.dot(
                (before * inverse).astype(jnp.bfloat16),
                v_ref[0, low:start, :],
                preferred_element_type=jnp.float32,
            )
        out_ref[0, start:stop, :] = result.astype(jnp.bfloat16)
        log_ref[0, start:stop, :] = jnp.broadcast_to(largest + jnp.log(total), (BLOCK, 128))


def attend_back_kernel(
    first_ref, q_ref, k_ref, v_ref, g_ref, log_ref, dq_ref, dk_ref, dv_ref, key_sum, value_sum
):
    group_len = q_ref.shape[1]
    scale = 1.0 / math.sqrt(HEAD_DIM)
    key_sum[...] = jnp.zeros_like(key_sum)
    value_sum[...] = jnp.zeros_like(value_sum)
    for number in range(group_len // BLOCK):
        start, low = window(number)
        stop = start + BLOCK
        query = q_ref[0, start:stop, :]
        grad = g_ref[0, start:stop, :]
        log_total = log_ref[0, start:stop, 0:1]
        scores = block_scores(query, k_ref, first_ref, start, low)
        parts = []
        weighted = None
        for part, begin, end in ((scores[0], start, stop), (scores[1], low, start)):
            if part is None:
                continue
            probs = jnp.exp(part - log_total)
            grad_probs = contract_last(grad, v_ref[0, begin:end, :])
            term = jnp.sum(probs * grad_probs, axis=1, keepdims=True)
            weighted = term if weighted is None else weighted + term
            parts.append((probs, grad_probs, begin, end))
        grad_query = None
        for probs, grad_probs, begin, end in parts:
            grad_scores = (probs * (grad_probs - weighted)).astype(jnp.bfloat16)
            term = jnp.dot(grad_scores, k_ref[0, begin:end, :], preferred_element_type=jnp.float32)
            grad_query = term if grad_query is None else grad_query + term
            key_sum[begin:end, :] += contract_first(grad_scores, query)
            value_sum[begin:end, :] += contract_first(probs.astype(jnp.bfloat16), grad)
        dq_ref[0, start:stop, :] = (grad_query * scale).astype(jnp.bfloat16)
    dk_ref[0] = key_sum[...].astype(jnp.bfloat16)
    dv_ref[0] = value_sum[...].astype(jnp.bfloat16)


def head_spec(group_len, width, offset=0):
    return pl.BlockSpec((1, group_len, width), lambda head: (head + offset, 0, 0))


def attend(first, heads_in):
    head_count, group_len, width = heads_in.shape
    head_count = head_count // 3
    return pl.pallas_call(
        attend_kernel,
        grid=(head_count,),
        in_specs=[pl.BlockSpec((group_len, 128), lambda head: (0, 0))]
        + [head_spec(group_len, width, head_count * part) for part in range(3)],
        out_specs=[head_spec(group_len, width), head_spec(group_len, 128)],
        out_shape=[
            jax.ShapeDtypeStruct((head_count, group_len, width), jnp.bfloat16),
            jax.ShapeDtypeStruct((head_count, group_len, 128), jnp.float32),
        ],
        compiler_params=pltpu.CompilerParams(vmem_limit_bytes=VMEM_BYTES),
        cost_estimate=pl.CostEstimate(
            flops=head_count * group_len * 1280 * 256,
            bytes_accessed=head_count * group_len * 1536,
            transcendentals=head_count * group_len * 1280,
        ),
    )(first, heads_in, heads_in, heads_in)


def attend_back(first, heads_in, grad_out, log_total):
    head_count, group_len, width = grad_out.shape
    like = jax.ShapeDtypeStruct((head_count, group_len, width), jnp.bfloat16)
    return pl.pallas_call(
        attend_back_kernel,
        grid=(head_count,),
        in_specs=[pl.BlockSpec((group_len, 128), lambda head: (0, 0))]
        + [head_spec(group_len, width, head_count * part) for part in range(3)]
        + [head_spec(group_len, width), head_spec(group_len, 128)],
        out_specs=[head_spec(group_len, width)] * 3,
        out_shape=[like] * 3,
        scratch_shapes=[pltpu.VMEM((group_len, width), jnp.float32)] * 2,
        compiler_params=pltpu.CompilerParams(vmem_limit_bytes=VMEM_BYTES),
        cost_estimate=pl.CostEstimate(
            flops=head_count * group_len * 1280 * 640,
            bytes_accessed=head_count * group_len * 2048,
            transcendentals=head_count * group_len * 1280,
        ),
    )(first, heads_in, heads_in, heads_in, grad_out, log_total)


def gather(values, axis_name, axis=0):
    return lax.all_gather(values, axis_name, axis=axis, tiled=True)


def scatter_sum(values, axis_name, axis=0):
    return lax.psum_scatter(values, axis_name, scatter_dimension=axis, tiled=True)


def local(
    tokens,
    ln1_gain,
    ln1_bias,
    w_qkv,
    bias_qv,
    w_out,
    bias_out,
    ln2_gain,
    ln2_bias,
    w_in,
    bias_in,
    w_back,
    bias_back,
    seq_lengths,
    cotangent,
):
    low, full = jnp.bfloat16, jnp.float32
    tok_count, width = tokens.shape[1], tokens.shape[2]
    parts = lax.axis_size("heads")
    mine = lax.axis_index("heads")
    part_width = width // parts
    head_count = part_width // HEAD_DIM
    shard_rows = w_qkv.shape[0]

    group_tokens = gather(tokens[0], "heads")
    group_len = group_tokens.shape[0]
    own_qkv = lax.dynamic_slice_in_dim(
        w_qkv.reshape(shard_rows, 3, width), mine * part_width, part_width, 2
    ).reshape(shard_rows, 3 * part_width)
    own_qkv = gather(own_qkv, "shard")
    vectors = gather(
        jnp.concatenate(
            [
                jnp.stack([ln1_gain, ln1_bias, bias_out, ln2_gain, ln2_bias, bias_back]),
                bias_qv,
            ]
        ),
        "shard",
        1,
    ).astype(full)
    gain_one, shift_one, out_bias, gain_two, shift_two, back_bias = (vectors[i] for i in range(6))
    full_out = gather(w_out, "shard")
    full_in = gather(gather(w_in, "tensor"), "shard")
    full_back = gather(gather(w_back, "tensor"), "shard")
    in_bias = gather(gather(bias_in, "tensor"), "shard").astype(full)

    inputs = tokens[0].astype(full)
    _, norm_one_back = jax.vjp(layer_norm, inputs, gain_one, shift_one)
    attn_in = layer_norm(group_tokens.astype(full), gain_one, shift_one).astype(low)
    own_bias = lax.dynamic_slice_in_dim(vectors[6:8], mine * part_width, part_width, 1)
    qkv_bias = jnp.concatenate([own_bias[0], jnp.zeros((part_width,), full), own_bias[1]])
    projected = (jnp.dot(attn_in, own_qkv, preferred_element_type=full) + qkv_bias).astype(low)
    shrink = jnp.where(jnp.arange(3 * part_width) < part_width, 1.0 / math.sqrt(HEAD_DIM), 1.0)
    heads_in = (
        (projected * shrink.astype(low))
        .reshape(group_len, 3 * head_count, HEAD_DIM)
        .transpose(1, 0, 2)
    )
    first = jnp.broadcast_to(
        sequence_starts(seq_lengths[0], group_len)[:, None], (group_len, 128)
    )
    attended, log_total = attend(first, heads_in)
    attended = attended.transpose(1, 0, 2).reshape(group_len, part_width)
    back_tok = lax.all_to_all(attended, "heads", split_axis=0, concat_axis=1, tiled=True)
    hidden_res = inputs + jnp.dot(back_tok, full_out, preferred_element_type=full) + out_bias

    normed_two, norm_two_back = jax.vjp(layer_norm, hidden_res, gain_two, shift_two)
    mlp_in = normed_two.astype(low)
    cot_rows = cotangent[0]
    cot_float = cot_rows.astype(full)
    pre_act = contract_last(mlp_in, full_in) + in_bias
    activated, gelu_back = jax.vjp(gelu_tanh, pre_act)
    act_low = activated.astype(low)
    branch = jnp.dot(act_low, full_back, preferred_element_type=full)
    output = (hidden_res + branch + back_bias).astype(low)[None]
    grad_w_back = contract_first(act_low, cot_rows).astype(low)
    grad_act = contract_last(cot_rows, full_back)
    grad_pre = gelu_back(grad_act)[0].astype(low)
    grad_in_bias = jnp.sum(grad_pre.astype(full), axis=0)
    grad_w_in = contract_first(grad_pre, mlp_in).astype(low)
    grad_normed_two = jnp.dot(grad_pre, full_in, preferred_element_type=full)
    grad_res_norm, grad_gain_two, grad_shift_two = norm_two_back(grad_normed_two)
    grad_hidden = cot_float + grad_res_norm
    hidden_low = grad_hidden.astype(low)
    grad_w_out = contract_first(back_tok, hidden_low).astype(low)

    grad_attended = contract_last(hidden_low, full_out).astype(low)
    grad_heads = lax.all_to_all(grad_attended, "heads", split_axis=1, concat_axis=0, tiled=True)
    grad_heads = grad_heads.reshape(group_len, head_count, HEAD_DIM).transpose(1, 0, 2)
    grads = attend_back(first, heads_in, grad_heads, log_total)
    grad_proj = (
        jnp.concatenate(grads, axis=0).transpose(1, 0, 2).reshape(group_len, 3 * part_width)
    )
    grad_attn_in = scatter_sum(contract_last(grad_proj, own_qkv).astype(low), "heads").astype(full)
    grad_w_qkv = contract_first(attn_in, grad_proj).astype(low)
    grad_proj_sum = jnp.sum(grad_proj.astype(full), axis=0).reshape(3, part_width)
    grad_qv_bias = lax.dynamic_update_slice_in_dim(
        jnp.zeros((2, width), full), grad_proj_sum[0::2], mine * part_width, 1
    )
    grad_input_norm, grad_gain_one, grad_shift_one = norm_one_back(grad_attn_in)
    input_grad = (grad_hidden + grad_input_norm).astype(low)[None]

    own_back = lax.psum(scatter_sum(scatter_sum(grad_w_back, "shard"), "tensor"), "heads")
    own_in = lax.psum(scatter_sum(scatter_sum(grad_w_in, "shard"), "tensor"), "heads")
    own_out = lax.psum(scatter_sum(grad_w_out, "shard"), ("heads", "tensor"))
    part_qkv = lax.psum(scatter_sum(grad_w_qkv, "shard"), "tensor")
    own_grad_qkv = (
        lax.all_gather(part_qkv.reshape(shard_rows, 3, part_width), "heads", axis=2, tiled=True)
        .reshape(shard_rows, 3 * width)
        .astype(full)
    )
    sums = lax.psum(
        jnp.concatenate(
            [
                jnp.stack(
                    [
                        grad_gain_one,
                        grad_shift_one,
                        jnp.sum(hidden_low.astype(full), axis=0),
                        grad_gain_two,
                        grad_shift_two,
                        jnp.sum(cot_float, axis=0),
                    ]
                ),
                grad_qv_bias,
                grad_in_bias.reshape(-1, width),
            ]
        ),
        ("shard", "heads", "tensor"),
    )
    shard = lax.axis_index("shard")
    owned = lax.dynamic_slice_in_dim(sums[:8], shard * shard_rows, shard_rows, 1)
    hidden_rows = bias_in.shape[0]
    place = shard * lax.axis_size("tensor") + lax.axis_index("tensor")
    own_in_bias = lax.dynamic_slice_in_dim(
        sums[8:].reshape(-1), place * hidden_rows, hidden_rows, 0
    )
    return (
        output,
        input_grad,
        owned[0],
        owned[1],
        own_grad_qkv,
        owned[6:8],
        own_out.astype(full),
        owned[2],
        owned[3],
        owned[4],
        own_in.astype(full),
        own_in_bias,
        own_back.astype(full),
        owned[5],
    )


def solution(mesh):
    in_specs = (
        P(("shard", "tensor"), "heads", None),
        P("shard"),
        P("shard"),
        P("shard", None),
        P(None, "shard"),
        P("shard", None),
        P("shard"),
        P("shard"),
        P("shard"),
        P(("shard", "tensor"), None),
        P(("shard", "tensor")),
        P(("shard", "tensor"), None),
        P("shard"),
        P(("shard", "tensor"), None),
        P(("shard", "tensor"), "heads", None),
    )
    out_specs = (
        P(("shard", "tensor"), "heads", None),
        P(("shard", "tensor"), "heads", None),
        P("shard"),
        P("shard"),
        P("shard", None),
        P(None, "shard"),
        P("shard", None),
        P("shard"),
        P("shard"),
        P("shard"),
        P(("shard", "tensor"), None),
        P(("shard", "tensor")),
        P(("shard", "tensor"), None),
        P("shard"),
    )
    return jax.shard_map(local, mesh=mesh, in_specs=in_specs, out_specs=out_specs, check_vma=False)
```

```python
import math

import jax
import jax.numpy as jnp
from jax import lax
from jax.experimental import pallas as pl
from jax.experimental.pallas import tpu as pltpu
from jax.sharding import PartitionSpec as P

HEAD_DIM = 64
BLOCK = 256
LONGEST = 1024
VMEM_BYTES = 48 * 1024 * 1024


EPSILON = 1e-05
NEGATIVE = -1e30


def layer_norm(values, gain, shift):
    center = jnp.mean(values, axis=-1, keepdims=True)
    offset = values - center
    spread = jnp.mean(offset * offset, axis=-1, keepdims=True)
    return offset * lax.rsqrt(spread + EPSILON) * gain + shift


def gelu_tanh(values):
    return jax.nn.gelu(values, approximate=True)


def contract_last(left, right):
    return lax.dot_general(
        left, right, (((1,), (1,)), ((), ())), preferred_element_type=jnp.float32
    )


def contract_first(left, right):
    return lax.dot_general(
        left, right, (((0,), (0,)), ((), ())), preferred_element_type=jnp.float32
    )


def sequence_starts(lengths, count):
    ends = jnp.cumsum(lengths)
    positions = jnp.arange(count, dtype=jnp.int32)
    past = ends[None, :] <= positions[:, None]
    return jnp.max(jnp.where(past, ends[None, :], 0), axis=1)


def window(number):
    start = number * BLOCK
    return start, max(0, start - LONGEST)


def block_scores(query, key_ref, first_ref, start, low):
    first = first_ref[start : start + BLOCK, 0:1]
    rows = lax.broadcasted_iota(jnp.int32, (BLOCK, BLOCK), 0)
    cols = lax.broadcasted_iota(jnp.int32, (BLOCK, BLOCK), 1)
    own = contract_last(query, key_ref[0, start : start + BLOCK, :])
    own = jnp.where((cols <= rows) & (cols >= first - start), own, NEGATIVE)
    if low == start:
        return own, None
    before = contract_last(query, key_ref[0, low:start, :])
    cols = lax.broadcasted_iota(jnp.int32, (BLOCK, start - low), 1)
    before = jnp.where(cols >= first - low, before, NEGATIVE)
    return own, before


def attend_kernel(first_ref, q_ref, k_ref, v_ref, out_ref, log_ref):
    group_len = q_ref.shape[1]
    for number in range(group_len // BLOCK):
        start, low = window(number)
        stop = start + BLOCK
        query = q_ref[0, start:stop, :]
        own, before = block_scores(query, k_ref, first_ref, start, low)
        largest = jnp.max(own, axis=1, keepdims=True)
        if before is not None:
            largest = jnp.maximum(largest, jnp.max(before, axis=1, keepdims=True))
        own = jnp.exp(own - largest)
        total = jnp.sum(own, axis=1, keepdims=True)
        if before is not None:
            before = jnp.exp(before - largest)
            total = total + jnp.sum(before, axis=1, keepdims=True)
        inverse = 1.0 / total
        result = jnp.dot(
            (own * inverse).astype(jnp.bfloat16),
            v_ref[0, start:stop, :],
            preferred_element_type=jnp.float32,
        )
        if before is not None:
            result = result + jnp.dot(
                (before * inverse).astype(jnp.bfloat16),
                v_ref[0, low:start, :],
                preferred_element_type=jnp.float32,
            )
        out_ref[0, start:stop, :] = result.astype(jnp.bfloat16)
        log_ref[0, start:stop, :] = jnp.broadcast_to(largest + jnp.log(total), (BLOCK, 128))


def attend_back_kernel(
    first_ref, q_ref, k_ref, v_ref, g_ref, log_ref, dq_ref, dk_ref, dv_ref, key_sum, value_sum
):
    group_len = q_ref.shape[1]
    scale = 1.0 / math.sqrt(HEAD_DIM)
    key_sum[...] = jnp.zeros_like(key_sum)
    value_sum[...] = jnp.zeros_like(value_sum)
    for number in range(group_len // BLOCK):
        start, low = window(number)
        stop = start + BLOCK
        query = q_ref[0, start:stop, :]
        grad = g_ref[0, start:stop, :]
        log_total = log_ref[0, start:stop, 0:1]
        scores = block_scores(query, k_ref, first_ref, start, low)
        parts = []
        weighted = None
        for part, begin, end in ((scores[0], start, stop), (scores[1], low, start)):
            if part is None:
                continue
            probs = jnp.exp(part - log_total)
            grad_probs = contract_last(grad, v_ref[0, begin:end, :])
            term = jnp.sum(probs * grad_probs, axis=1, keepdims=True)
            weighted = term if weighted is None else weighted + term
            parts.append((probs, grad_probs, begin, end))
        grad_query = None
        for probs, grad_probs, begin, end in parts:
            grad_scores = (probs * (grad_probs - weighted)).astype(jnp.bfloat16)
            term = jnp.dot(grad_scores, k_ref[0, begin:end, :], preferred_element_type=jnp.float32)
            grad_query = term if grad_query is None else grad_query + term
            key_sum[begin:end, :] += contract_first(grad_scores, query)
            value_sum[begin:end, :] += contract_first(probs.astype(jnp.bfloat16), grad)
        dq_ref[0, start:stop, :] = (grad_query * scale).astype(jnp.bfloat16)
    dk_ref[0] = key_sum[...].astype(jnp.bfloat16)
    dv_ref[0] = value_sum[...].astype(jnp.bfloat16)


def head_spec(group_len, width, offset=0):
    return pl.BlockSpec((1, group_len, width), lambda head: (head + offset, 0, 0))


def attend(first, heads_in):
    head_count, group_len, width = heads_in.shape
    head_count = head_count // 3
    return pl.pallas_call(
        attend_kernel,
        grid=(head_count,),
        in_specs=[pl.BlockSpec((group_len, 128), lambda head: (0, 0))]
        + [head_spec(group_len, width, head_count * part) for part in range(3)],
        out_specs=[head_spec(group_len, width), head_spec(group_len, 128)],
        out_shape=[
            jax.ShapeDtypeStruct((head_count, group_len, width), jnp.bfloat16),
            jax.ShapeDtypeStruct((head_count, group_len, 128), jnp.float32),
        ],
        compiler_params=pltpu.CompilerParams(vmem_limit_bytes=VMEM_BYTES),
        cost_estimate=pl.CostEstimate(
            flops=head_count * group_len * 1280 * 256,
            bytes_accessed=head_count * group_len * 1536,
            transcendentals=head_count * group_len * 1280,
        ),
    )(first, heads_in, heads_in, heads_in)


def attend_back(first, heads_in, grad_out, log_total):
    head_count, group_len, width = grad_out.shape
    like = jax.ShapeDtypeStruct((head_count, group_len, width), jnp.bfloat16)
    return pl.pallas_call(
        attend_back_kernel,
        grid=(head_count,),
        in_specs=[pl.BlockSpec((group_len, 128), lambda head: (0, 0))]
        + [head_spec(group_len, width, head_count * part) for part in range(3)]
        + [head_spec(group_len, width), head_spec(group_len, 128)],
        out_specs=[head_spec(group_len, width)] * 3,
        out_shape=[like] * 3,
        scratch_shapes=[pltpu.VMEM((group_len, width), jnp.float32)] * 2,
        compiler_params=pltpu.CompilerParams(vmem_limit_bytes=VMEM_BYTES),
        cost_estimate=pl.CostEstimate(
            flops=head_count * group_len * 1280 * 640,
            bytes_accessed=head_count * group_len * 2048,
            transcendentals=head_count * group_len * 1280,
        ),
    )(first, heads_in, heads_in, heads_in, grad_out, log_total)


def partner(axis_name, step):
    return lax.axis_index(axis_name) ^ step


def swap(values, axis_name, step):
    count = lax.axis_size(axis_name)
    return lax.ppermute(values, axis_name, [(i, i ^ step) for i in range(count)])


def direct(axis_name):
    count = lax.axis_size(axis_name)
    return count <= 4 and count & (count - 1) == 0


def gather_into(values, axis_name, axis=0):
    if not direct(axis_name):
        return lax.all_gather(values, axis_name, axis=axis)
    count = lax.axis_size(axis_name)
    shape = values.shape[:axis] + (count,) + values.shape[axis:]
    pieces = [swap(values, axis_name, step) for step in range(1, count)]
    whole = jnp.zeros(shape, values.dtype)
    for step, piece in enumerate([values] + pieces):
        whole = lax.dynamic_update_index_in_dim(whole, piece, partner(axis_name, step), axis)
    return whole


def gather(values, axis_name, axis=0):
    whole = gather_into(values, axis_name, axis)
    shape = list(values.shape)
    shape[axis] *= lax.axis_size(axis_name)
    return whole.reshape(shape)


def exchange(values, axis_name, split, join):
    if not direct(axis_name):
        moved = jnp.moveaxis(values, split, 0)
        moved = lax.all_to_all(moved, axis_name, split_axis=0, concat_axis=0, tiled=True)
        return jnp.moveaxis(moved, 0, join)
    pieces = []
    for step in range(lax.axis_size(axis_name)):
        piece = lax.dynamic_index_in_dim(values, partner(axis_name, step), split, keepdims=False)
        pieces.append(swap(piece, axis_name, step) if step else piece)
    shape = pieces[0].shape
    whole = jnp.zeros(shape[:join] + (len(pieces),) + shape[join:], values.dtype)
    for step, piece in enumerate(pieces):
        whole = lax.dynamic_update_index_in_dim(whole, piece, partner(axis_name, step), join)
    return whole


def scatter_sum(values, axis_name, split=0):
    if not direct(axis_name):
        total = lax.psum_scatter(values, axis_name, scatter_dimension=split, tiled=False)
        return total.astype(jnp.float32)
    total = None
    for step in reversed(range(lax.axis_size(axis_name))):
        piece = lax.dynamic_index_in_dim(values, partner(axis_name, step), split, keepdims=False)
        piece = (swap(piece, axis_name, step) if step else piece).astype(jnp.float32)
        total = piece if total is None else total + piece
    return total


def small_sum(values, axis_names):
    for axis_name in axis_names:
        count = lax.axis_size(axis_name)
        if count & (count - 1):
            values = lax.psum(values, axis_name)
            continue
        step = 1
        while step < count:
            values = values + swap(values, axis_name, step)
            step *= 2
    return values


def halves(values):
    if lax.axis_size("shard") == 2:
        return [values, swap(values, "shard", 1)]
    return [lax.all_gather(values, "shard", axis=0, tiled=True)]


def sum_halves(grads):
    if len(grads) == 2:
        received = swap(grads[1].astype(jnp.bfloat16), "shard", 1)
        return (grads[0] + received.astype(jnp.float32)).astype(jnp.bfloat16)
    return lax.psum_scatter(
        grads[0].astype(jnp.bfloat16), "shard", scatter_dimension=0, tiled=True
    )


def shard_rows_sum(values):
    shards = lax.axis_size("shard")
    split = values.reshape((shards, values.shape[0] // shards) + values.shape[1:])
    return scatter_sum(split, "shard").astype(jnp.bfloat16)


def local(
    tokens,
    ln1_gain,
    ln1_bias,
    w_qkv,
    bias_qv,
    w_out,
    bias_out,
    ln2_gain,
    ln2_bias,
    w_in,
    bias_in,
    w_back,
    bias_back,
    seq_lengths,
    cotangent,
):
    low, full = jnp.bfloat16, jnp.float32
    tok_count, width = tokens.shape[1], tokens.shape[2]
    parts = lax.axis_size("heads")
    depth = lax.axis_size("tensor")
    mine = lax.axis_index("heads")
    part_width = width // parts
    head_count = part_width // HEAD_DIM
    shard_rows = w_qkv.shape[0]
    hidden_rows = w_in.shape[0]
    quarter = hidden_rows // parts

    group_tokens = gather(tokens[0], "heads")
    group_len = group_tokens.shape[0]
    own_qkv = lax.dynamic_slice_in_dim(
        w_qkv.reshape(shard_rows, 3, width), mine * part_width, part_width, 2
    ).reshape(shard_rows, 3 * part_width)
    own_qkv = gather(own_qkv, "shard")
    vectors = gather(
        jnp.concatenate(
            [
                jnp.stack([ln1_gain, ln1_bias, bias_out, ln2_gain, ln2_bias, bias_back]),
                bias_qv,
            ]
        ),
        "shard",
        1,
    ).astype(full)
    gain_one, shift_one, out_bias, gain_two, shift_two, back_bias = (vectors[i] for i in range(6))
    full_out = gather(w_out, "shard")

    back_quarter = lax.dynamic_slice_in_dim(w_back, mine * quarter, quarter, 0)
    back_quarter = lax.all_gather(back_quarter, "tensor", axis=0)
    w_in, back_quarter = lax.optimization_barrier((w_in, back_quarter))
    in_parts = halves(lax.all_gather(w_in, "tensor", axis=0, tiled=True))
    bias_parts = halves(gather(bias_in, "tensor"))

    inputs = tokens[0].astype(full)
    _, norm_one_back = jax.vjp(layer_norm, inputs, gain_one, shift_one)
    attn_in = layer_norm(group_tokens.astype(full), gain_one, shift_one).astype(low)
    own_bias = lax.dynamic_slice_in_dim(vectors[6:8], mine * part_width, part_width, 1)
    qkv_bias = jnp.concatenate([own_bias[0], jnp.zeros((part_width,), full), own_bias[1]])
    projected = (jnp.dot(attn_in, own_qkv, preferred_element_type=full) + qkv_bias).astype(low)
    back_quarter, projected = lax.optimization_barrier((back_quarter, projected))
    back_parts = halves(gather_into(back_quarter, "heads", 1).reshape(-1, width))
    shrink = jnp.where(jnp.arange(3 * part_width) < part_width, 1.0 / math.sqrt(HEAD_DIM), 1.0)
    heads_in = (
        (projected * shrink.astype(low))
        .reshape(group_len, 3 * head_count, HEAD_DIM)
        .transpose(1, 0, 2)
    )
    first = jnp.broadcast_to(
        sequence_starts(seq_lengths[0], group_len)[:, None], (group_len, 128)
    )
    attended, log_total = attend(first, heads_in)
    attended = attended.transpose(1, 0, 2).reshape(parts, tok_count, part_width)
    back_tok = exchange(attended, "heads", 0, 1).reshape(tok_count, width)
    hidden_res = inputs + jnp.dot(back_tok, full_out, preferred_element_type=full) + out_bias

    normed_two, norm_two_back = jax.vjp(layer_norm, hidden_res, gain_two, shift_two)
    mlp_in = normed_two.astype(low)
    cot_rows = cotangent[0]
    cot_float = cot_rows.astype(full)
    result = hidden_res + back_bias
    grad_normed_two = 0.0
    grads_back, grads_in, grads_bias = [], [], []
    for part_in, part_bias, part_back in zip(in_parts, bias_parts, back_parts):
        pre_act = contract_last(mlp_in, part_in) + part_bias.astype(full)
        activated, gelu_back = jax.vjp(gelu_tanh, pre_act)
        act_low = activated.astype(low)
        result = result + jnp.dot(act_low, part_back, preferred_element_type=full)
        grads_back.append(contract_first(act_low, cot_rows))
        grad_pre = gelu_back(contract_last(cot_rows, part_back))[0].astype(low)
        grads_bias.append(jnp.sum(grad_pre.astype(full), axis=0))
        grads_in.append(contract_first(grad_pre, mlp_in))
        grad_normed_two += jnp.dot(grad_pre, part_in, preferred_element_type=full)
    output = result.astype(low)[None]
    grad_res_norm, grad_gain_two, grad_shift_two = norm_two_back(grad_normed_two)
    grad_hidden = cot_float + grad_res_norm
    hidden_low = grad_hidden.astype(low)
    grad_w_out = contract_first(back_tok, hidden_low).astype(low)

    grad_attended = contract_last(hidden_low, full_out).astype(low)
    grad_heads = exchange(grad_attended.reshape(tok_count, parts, part_width), "heads", 1, 0)
    sum_back, sum_in, sum_out = (
        sum_halves(grads_back),
        sum_halves(grads_in),
        shard_rows_sum(grad_w_out),
    )
    grad_heads, sum_back, sum_in, sum_out = lax.optimization_barrier(
        (grad_heads, sum_back, sum_in, sum_out)
    )
    by_part = (depth, parts, quarter, width)
    part_back = scatter_sum(sum_back.reshape(by_part), "heads", 1)
    part_in = scatter_sum(sum_in.reshape(by_part), "heads", 1)
    part_out = scatter_sum(sum_out.reshape(parts, shard_rows // parts, width), "heads", 0)
    grad_heads = grad_heads.reshape(group_len, head_count, HEAD_DIM).transpose(1, 0, 2)
    grads = attend_back(first, heads_in, grad_heads, log_total)
    grads, part_back, part_in, part_out = lax.optimization_barrier(
        (grads, part_back.astype(low), part_in.astype(low), part_out.astype(low))
    )
    own_pair = lax.psum_scatter(
        jnp.concatenate([part_back, part_in], axis=1),
        "tensor",
        scatter_dimension=0,
        tiled=False,
    )
    part_out = lax.psum(part_out, "tensor")
    grad_proj = (
        jnp.concatenate(grads, axis=0).transpose(1, 0, 2).reshape(group_len, 3 * part_width)
    )
    grad_w_qkv = shard_rows_sum(contract_first(attn_in, grad_proj).astype(low))
    grad_attn_in = contract_last(grad_proj, own_qkv).astype(low)
    grad_attn_in = scatter_sum(grad_attn_in.reshape(parts, tok_count, width), "heads")
    grad_attn_in, own_pair, part_out = lax.optimization_barrier((grad_attn_in, own_pair, part_out))
    own_three = gather_into(jnp.concatenate([own_pair, part_out], axis=0), "heads", 0)
    own_back = own_three[:, :quarter].reshape(hidden_rows, width)
    own_in = own_three[:, quarter : 2 * quarter].reshape(hidden_rows, width)
    own_out = own_three[:, 2 * quarter :].reshape(shard_rows, width)

    part_qkv = scatter_sum(
        grad_w_qkv.reshape(depth, shard_rows // depth, 3 * part_width), "tensor"
    ).astype(low)
    part_qkv = gather(part_qkv, "tensor").reshape(shard_rows, 3, part_width)
    own_grad_qkv = gather_into(part_qkv, "heads", 2).reshape(shard_rows, 3 * width)
    grad_proj_sum = jnp.sum(grad_proj.astype(full), axis=0).reshape(3, part_width)
    grad_qv_bias = lax.dynamic_update_slice_in_dim(
        jnp.zeros((2, width), full), grad_proj_sum[0::2], mine * part_width, 1
    )
    grad_input_norm, grad_gain_one, grad_shift_one = norm_one_back(grad_attn_in)
    input_grad = (grad_hidden + grad_input_norm).astype(low)[None]

    shard = lax.axis_index("shard")
    if len(grads_bias) == 2:
        ordered = jnp.zeros((2, grads_bias[0].shape[0]), full)
        ordered = lax.dynamic_update_index_in_dim(ordered, grads_bias[0], shard, 0)
        grad_in_bias = lax.dynamic_update_index_in_dim(ordered, grads_bias[1], 1 - shard, 0)
    else:
        grad_in_bias = grads_bias[0]
    sums = small_sum(
        jnp.concatenate(
            [
                jnp.stack(
                    [
                        grad_gain_one,
                        grad_shift_one,
                        jnp.sum(hidden_low.astype(full), axis=0),
                        grad_gain_two,
                        grad_shift_two,
                        jnp.sum(cot_float, axis=0),
                    ]
                ),
                grad_qv_bias,
                grad_in_bias.reshape(-1, width),
            ]
        ),
        ("shard", "heads", "tensor"),
    )
    owned = lax.dynamic_slice_in_dim(sums[:8], shard * shard_rows, shard_rows, 1)
    place = shard * depth + lax.axis_index("tensor")
    own_in_bias = lax.dynamic_slice_in_dim(
        sums[8:].reshape(-1), place * hidden_rows, hidden_rows, 0
    )
    return (
        output,
        input_grad,
        owned[0],
        owned[1],
        own_grad_qkv.astype(full),
        owned[6:8],
        own_out.astype(full),
        owned[2],
        owned[3],
        owned[4],
        own_in.astype(full),
        own_in_bias,
        own_back.astype(full),
        owned[5],
    )


def solution(mesh):
    in_specs = (
        P(("shard", "tensor"), "heads", None),
        P("shard"),
        P("shard"),
        P("shard", None),
        P(None, "shard"),
        P("shard", None),
        P("shard"),
        P("shard"),
        P("shard"),
        P(("shard", "tensor"), None),
        P(("shard", "tensor")),
        P(("shard", "tensor"), None),
        P("shard"),
        P(("shard", "tensor"), None),
        P(("shard", "tensor"), "heads", None),
    )
    out_specs = (
        P(("shard", "tensor"), "heads", None),
        P(("shard", "tensor"), "heads", None),
        P("shard"),
        P("shard"),
        P("shard", None),
        P(None, "shard"),
        P("shard", None),
        P("shard"),
        P("shard"),
        P("shard"),
        P(("shard", "tensor"), None),
        P(("shard", "tensor")),
        P(("shard", "tensor"), None),
        P("shard"),
    )
    return jax.shard_map(local, mesh=mesh, in_specs=in_specs, out_specs=out_specs, check_vma=False)
```

```python
import math

import jax
import jax.numpy as jnp
from jax import lax
from jax.experimental import pallas as pl
from jax.experimental.pallas import tpu as pltpu
from jax.sharding import PartitionSpec as P

HEAD_DIM = 64
BLOCK = 256
LONGEST = 1024
VMEM_BYTES = 48 * 1024 * 1024


EPSILON = 1e-05
NEGATIVE = -1e30


def layer_norm(values, gain, shift):
    center = jnp.mean(values, axis=-1, keepdims=True)
    offset = values - center
    spread = jnp.mean(offset * offset, axis=-1, keepdims=True)
    return offset * lax.rsqrt(spread + EPSILON) * gain + shift


def gelu_tanh(values):
    return jax.nn.gelu(values, approximate=True)


def contract_last(left, right):
    return lax.dot_general(
        left, right, (((1,), (1,)), ((), ())), preferred_element_type=jnp.float32
    )


def contract_first(left, right):
    return lax.dot_general(
        left, right, (((0,), (0,)), ((), ())), preferred_element_type=jnp.float32
    )


def sequence_starts(lengths, count):
    ends = jnp.cumsum(lengths)
    positions = jnp.arange(count, dtype=jnp.int32)
    past = ends[None, :] <= positions[:, None]
    return jnp.max(jnp.where(past, ends[None, :], 0), axis=1)


def window(number):
    start = number * BLOCK
    return start, max(0, start - LONGEST)


def block_scores(query, key_ref, first_ref, start, low):
    first = first_ref[start : start + BLOCK, 0:1]
    rows = lax.broadcasted_iota(jnp.int32, (BLOCK, BLOCK), 0)
    cols = lax.broadcasted_iota(jnp.int32, (BLOCK, BLOCK), 1)
    own = contract_last(query, key_ref[0, start : start + BLOCK, :])
    own = jnp.where((cols <= rows) & (cols >= first - start), own, NEGATIVE)
    if low == start:
        return own, None
    before = contract_last(query, key_ref[0, low:start, :])
    cols = lax.broadcasted_iota(jnp.int32, (BLOCK, start - low), 1)
    before = jnp.where(cols >= first - low, before, NEGATIVE)
    return own, before


def attend_kernel(first_ref, q_ref, k_ref, v_ref, out_ref, log_ref):
    group_len = q_ref.shape[1]
    for number in range(group_len // BLOCK):
        start, low = window(number)
        stop = start + BLOCK
        query = q_ref[0, start:stop, :]
        own, before = block_scores(query, k_ref, first_ref, start, low)
        largest = jnp.max(own, axis=1, keepdims=True)
        if before is not None:
            largest = jnp.maximum(largest, jnp.max(before, axis=1, keepdims=True))
        own = jnp.exp(own - largest)
        total = jnp.sum(own, axis=1, keepdims=True)
        if before is not None:
            before = jnp.exp(before - largest)
            total = total + jnp.sum(before, axis=1, keepdims=True)
        inverse = 1.0 / total
        result = jnp.dot(
            (own * inverse).astype(jnp.bfloat16),
            v_ref[0, start:stop, :],
            preferred_element_type=jnp.float32,
        )
        if before is not None:
            result = result + jnp.dot(
                (before * inverse).astype(jnp.bfloat16),
                v_ref[0, low:start, :],
                preferred_element_type=jnp.float32,
            )
        out_ref[0, start:stop, :] = result.astype(jnp.bfloat16)
        log_ref[0, start:stop, :] = jnp.broadcast_to(largest + jnp.log(total), (BLOCK, 128))


def attend_back_kernel(
    first_ref, q_ref, k_ref, v_ref, g_ref, log_ref, dq_ref, dk_ref, dv_ref, key_sum, value_sum
):
    group_len = q_ref.shape[1]
    scale = 1.0 / math.sqrt(HEAD_DIM)
    key_sum[...] = jnp.zeros_like(key_sum)
    value_sum[...] = jnp.zeros_like(value_sum)
    for number in range(group_len // BLOCK):
        start, low = window(number)
        stop = start + BLOCK
        query = q_ref[0, start:stop, :]
        grad = g_ref[0, start:stop, :]
        log_total = log_ref[0, start:stop, 0:1]
        scores = block_scores(query, k_ref, first_ref, start, low)
        parts = []
        weighted = None
        for part, begin, end in ((scores[0], start, stop), (scores[1], low, start)):
            if part is None:
                continue
            probs = jnp.exp(part - log_total)
            grad_probs = contract_last(grad, v_ref[0, begin:end, :])
            term = jnp.sum(probs * grad_probs, axis=1, keepdims=True)
            weighted = term if weighted is None else weighted + term
            parts.append((probs, grad_probs, begin, end))
        grad_query = None
        for probs, grad_probs, begin, end in parts:
            grad_scores = (probs * (grad_probs - weighted)).astype(jnp.bfloat16)
            term = jnp.dot(grad_scores, k_ref[0, begin:end, :], preferred_element_type=jnp.float32)
            grad_query = term if grad_query is None else grad_query + term
            key_sum[begin:end, :] += contract_first(grad_scores, query)
            value_sum[begin:end, :] += contract_first(probs.astype(jnp.bfloat16), grad)
        dq_ref[0, start:stop, :] = (grad_query * scale).astype(jnp.bfloat16)
    dk_ref[0] = key_sum[...].astype(jnp.bfloat16)
    dv_ref[0] = value_sum[...].astype(jnp.bfloat16)


def head_spec(group_len, width, offset=0):
    return pl.BlockSpec((1, group_len, width), lambda head: (head + offset, 0, 0))


def attend(first, heads_in):
    head_count, group_len, width = heads_in.shape
    head_count = head_count // 3
    return pl.pallas_call(
        attend_kernel,
        grid=(head_count,),
        in_specs=[pl.BlockSpec((group_len, 128), lambda head: (0, 0))]
        + [head_spec(group_len, width, head_count * part) for part in range(3)],
        out_specs=[head_spec(group_len, width), head_spec(group_len, 128)],
        out_shape=[
            jax.ShapeDtypeStruct((head_count, group_len, width), jnp.bfloat16),
            jax.ShapeDtypeStruct((head_count, group_len, 128), jnp.float32),
        ],
        compiler_params=pltpu.CompilerParams(vmem_limit_bytes=VMEM_BYTES),
        cost_estimate=pl.CostEstimate(
            flops=head_count * group_len * 1280 * 256,
            bytes_accessed=head_count * group_len * 1536,
            transcendentals=head_count * group_len * 1280,
        ),
    )(first, heads_in, heads_in, heads_in)


def attend_back(first, heads_in, grad_out, log_total):
    head_count, group_len, width = grad_out.shape
    like = jax.ShapeDtypeStruct((head_count, group_len, width), jnp.bfloat16)
    return pl.pallas_call(
        attend_back_kernel,
        grid=(head_count,),
        in_specs=[pl.BlockSpec((group_len, 128), lambda head: (0, 0))]
        + [head_spec(group_len, width, head_count * part) for part in range(3)]
        + [head_spec(group_len, width), head_spec(group_len, 128)],
        out_specs=[head_spec(group_len, width)] * 3,
        out_shape=[like] * 3,
        scratch_shapes=[pltpu.VMEM((group_len, width), jnp.float32)] * 2,
        compiler_params=pltpu.CompilerParams(vmem_limit_bytes=VMEM_BYTES),
        cost_estimate=pl.CostEstimate(
            flops=head_count * group_len * 1280 * 640,
            bytes_accessed=head_count * group_len * 2048,
            transcendentals=head_count * group_len * 1280,
        ),
    )(first, heads_in, heads_in, heads_in, grad_out, log_total)


def partner(axis_name, step):
    return lax.axis_index(axis_name) ^ step


def swap(values, axis_name, step):
    count = lax.axis_size(axis_name)
    return lax.ppermute(values, axis_name, [(i, i ^ step) for i in range(count)])


def direct(axis_name):
    count = lax.axis_size(axis_name)
    return count <= 4 and count & (count - 1) == 0


def in_order(pieces, axis_name, axis):
    mine = lax.axis_index(axis_name)
    bit = 1
    while bit < len(pieces):
        odd = (mine & bit) != 0
        pieces = [jnp.where(odd, pieces[i ^ bit], pieces[i]) for i in range(len(pieces))]
        bit *= 2
    return jnp.stack(pieces, axis=axis)


def gather_into(values, axis_name, axis=0):
    if not direct(axis_name):
        return lax.all_gather(values, axis_name, axis=axis)
    pieces = [swap(values, axis_name, step) for step in range(1, lax.axis_size(axis_name))]
    return in_order([values] + pieces, axis_name, axis)


def gather(values, axis_name, axis=0):
    whole = gather_into(values, axis_name, axis)
    shape = list(values.shape)
    shape[axis] *= lax.axis_size(axis_name)
    return whole.reshape(shape)


def exchange(values, axis_name, split, join):
    if not direct(axis_name):
        moved = jnp.moveaxis(values, split, 0)
        moved = lax.all_to_all(moved, axis_name, split_axis=0, concat_axis=0, tiled=True)
        return jnp.moveaxis(moved, 0, join)
    pieces = []
    for step in range(lax.axis_size(axis_name)):
        piece = lax.dynamic_index_in_dim(values, partner(axis_name, step), split, keepdims=False)
        pieces.append(swap(piece, axis_name, step) if step else piece)
    return in_order(pieces, axis_name, join)


def scatter_sum(values, axis_name, split=0):
    if not direct(axis_name):
        total = lax.psum_scatter(values, axis_name, scatter_dimension=split, tiled=False)
        return total.astype(jnp.float32)
    total = None
    for step in reversed(range(lax.axis_size(axis_name))):
        piece = lax.dynamic_index_in_dim(values, partner(axis_name, step), split, keepdims=False)
        piece = (swap(piece, axis_name, step) if step else piece).astype(jnp.float32)
        total = piece if total is None else total + piece
    return total


def small_sum(values, axis_names):
    for axis_name in axis_names:
        count = lax.axis_size(axis_name)
        if count & (count - 1):
            values = lax.psum(values, axis_name)
            continue
        step = 1
        while step < count:
            values = values + swap(values, axis_name, step)
            step *= 2
    return values


def halves(values):
    if lax.axis_size("shard") == 2:
        return [values, swap(values, "shard", 1)]
    return [lax.all_gather(values, "shard", axis=0, tiled=True)]


def sum_halves(grads):
    if len(grads) == 2:
        received = swap(grads[1].astype(jnp.bfloat16), "shard", 1)
        return (grads[0] + received.astype(jnp.float32)).astype(jnp.bfloat16)
    return lax.psum_scatter(
        grads[0].astype(jnp.bfloat16), "shard", scatter_dimension=0, tiled=True
    )


def shard_rows_sum(values):
    shards = lax.axis_size("shard")
    split = values.reshape((shards, values.shape[0] // shards) + values.shape[1:])
    return scatter_sum(split, "shard").astype(jnp.bfloat16)


def local(
    tokens,
    ln1_gain,
    ln1_bias,
    w_qkv,
    bias_qv,
    w_out,
    bias_out,
    ln2_gain,
    ln2_bias,
    w_in,
    bias_in,
    w_back,
    bias_back,
    seq_lengths,
    cotangent,
):
    low, full = jnp.bfloat16, jnp.float32
    tok_count, width = tokens.shape[1], tokens.shape[2]
    parts = lax.axis_size("heads")
    depth = lax.axis_size("tensor")
    mine = lax.axis_index("heads")
    part_width = width // parts
    head_count = part_width // HEAD_DIM
    shard_rows = w_qkv.shape[0]
    hidden_rows = w_in.shape[0]
    quarter = hidden_rows // parts

    group_tokens = gather(tokens[0], "heads")
    group_len = group_tokens.shape[0]
    own_qkv = lax.dynamic_slice_in_dim(
        w_qkv.reshape(shard_rows, 3, width), mine * part_width, part_width, 2
    ).reshape(shard_rows, 3 * part_width)
    own_qkv = gather(own_qkv, "shard")
    vectors = gather(
        jnp.concatenate(
            [
                jnp.stack([ln1_gain, ln1_bias, bias_out, ln2_gain, ln2_bias, bias_back]),
                bias_qv,
            ]
        ),
        "shard",
        1,
    ).astype(full)
    gain_one, shift_one, out_bias, gain_two, shift_two, back_bias = (vectors[i] for i in range(6))
    full_out = gather(w_out, "shard")

    back_quarter = lax.dynamic_slice_in_dim(w_back, mine * quarter, quarter, 0)
    back_quarter = gather_into(back_quarter, "tensor")
    in_parts = halves(lax.all_gather(w_in, "tensor", axis=0, tiled=True))
    bias_parts = halves(gather(bias_in, "tensor"))

    inputs = tokens[0].astype(full)
    _, norm_one_back = jax.vjp(layer_norm, inputs, gain_one, shift_one)
    attn_in = layer_norm(group_tokens.astype(full), gain_one, shift_one).astype(low)
    own_bias = lax.dynamic_slice_in_dim(vectors[6:8], mine * part_width, part_width, 1)
    qkv_bias = jnp.concatenate([own_bias[0], jnp.zeros((part_width,), full), own_bias[1]])
    projected = (jnp.dot(attn_in, own_qkv, preferred_element_type=full) + qkv_bias).astype(low)
    back_quarter, projected = lax.optimization_barrier((back_quarter, projected))
    back_parts = halves(gather_into(back_quarter, "heads", 1).reshape(-1, width))
    shrink = jnp.where(jnp.arange(3 * part_width) < part_width, 1.0 / math.sqrt(HEAD_DIM), 1.0)
    heads_in = (
        (projected * shrink.astype(low))
        .reshape(group_len, 3 * head_count, HEAD_DIM)
        .transpose(1, 0, 2)
    )
    first = jnp.broadcast_to(
        sequence_starts(seq_lengths[0], group_len)[:, None], (group_len, 128)
    )
    attended, log_total = attend(first, heads_in)
    attended = attended.transpose(1, 0, 2).reshape(parts, tok_count, part_width)
    back_tok = exchange(attended, "heads", 0, 1).reshape(tok_count, width)
    hidden_res = inputs + jnp.dot(back_tok, full_out, preferred_element_type=full) + out_bias

    normed_two, norm_two_back = jax.vjp(layer_norm, hidden_res, gain_two, shift_two)
    mlp_in = normed_two.astype(low)
    cot_rows = cotangent[0]
    cot_float = cot_rows.astype(full)
    result = hidden_res + back_bias
    grad_normed_two = 0.0
    grads_back, grads_in, grads_bias = [], [], []
    for part_in, part_bias, part_back in zip(in_parts, bias_parts, back_parts):
        pre_act = contract_last(mlp_in, part_in) + part_bias.astype(full)
        activated, gelu_back = jax.vjp(gelu_tanh, pre_act)
        act_low = activated.astype(low)
        result = result + jnp.dot(act_low, part_back, preferred_element_type=full)
        grads_back.append(contract_first(act_low, cot_rows))
        grad_pre = gelu_back(contract_last(cot_rows, part_back))[0].astype(low)
        grads_bias.append(jnp.sum(grad_pre.astype(full), axis=0))
        grads_in.append(contract_first(grad_pre, mlp_in))
        grad_normed_two += jnp.dot(grad_pre, part_in, preferred_element_type=full)
    output = result.astype(low)[None]
    grad_res_norm, grad_gain_two, grad_shift_two = norm_two_back(grad_normed_two)
    grad_hidden = cot_float + grad_res_norm
    hidden_low = grad_hidden.astype(low)
    grad_w_out = contract_first(back_tok, hidden_low).astype(low)

    grad_attended = contract_last(hidden_low, full_out).astype(low)
    grad_heads = exchange(grad_attended.reshape(tok_count, parts, part_width), "heads", 1, 0)
    sum_back, sum_in, sum_out = (
        sum_halves(grads_back),
        sum_halves(grads_in),
        shard_rows_sum(grad_w_out),
    )
    grad_heads, sum_back, sum_in, sum_out = lax.optimization_barrier(
        (grad_heads, sum_back, sum_in, sum_out)
    )
    by_part = (depth, parts, quarter, width)
    part_back = scatter_sum(sum_back.reshape(by_part), "heads", 1)
    part_in = scatter_sum(sum_in.reshape(by_part), "heads", 1)
    grad_heads = grad_heads.reshape(group_len, head_count, HEAD_DIM).transpose(1, 0, 2)
    grads = attend_back(first, heads_in, grad_heads, log_total)
    grads, part_back, part_in, sum_out = lax.optimization_barrier(
        (grads, part_back.astype(low), part_in.astype(low), sum_out)
    )
    part_out = scatter_sum(sum_out.reshape(parts, shard_rows // parts, width), "heads", 0)
    own_pair = lax.psum_scatter(
        jnp.concatenate([part_back, part_in], axis=1),
        "tensor",
        scatter_dimension=0,
        tiled=False,
    )
    part_out = lax.psum(part_out.astype(low), "tensor")
    grad_proj = (
        jnp.concatenate(grads, axis=0).transpose(1, 0, 2).reshape(group_len, 3 * part_width)
    )
    grad_w_qkv = shard_rows_sum(contract_first(attn_in, grad_proj).astype(low))
    grad_attn_in = contract_last(grad_proj, own_qkv).astype(low)
    grad_attn_in = scatter_sum(grad_attn_in.reshape(parts, tok_count, width), "heads")
    grad_attn_in, own_pair, part_out = lax.optimization_barrier((grad_attn_in, own_pair, part_out))
    own_three = gather_into(jnp.concatenate([own_pair, part_out], axis=0), "heads", 0)
    own_back = own_three[:, :quarter].reshape(hidden_rows, width)
    own_in = own_three[:, quarter : 2 * quarter].reshape(hidden_rows, width)
    own_out = own_three[:, 2 * quarter :].reshape(shard_rows, width)

    part_qkv = scatter_sum(
        grad_w_qkv.reshape(depth, shard_rows // depth, 3 * part_width), "tensor"
    ).astype(low)
    part_qkv = gather(part_qkv, "tensor").reshape(shard_rows, 3, part_width)
    own_grad_qkv = gather_into(part_qkv, "heads", 2).reshape(shard_rows, 3 * width)
    grad_proj_sum = jnp.sum(grad_proj.astype(full), axis=0).reshape(3, part_width)
    grad_qv_bias = lax.dynamic_update_slice_in_dim(
        jnp.zeros((2, width), full), grad_proj_sum[0::2], mine * part_width, 1
    )
    grad_input_norm, grad_gain_one, grad_shift_one = norm_one_back(grad_attn_in)
    input_grad = (grad_hidden + grad_input_norm).astype(low)[None]

    shard = lax.axis_index("shard")
    if len(grads_bias) == 2:
        ordered = jnp.zeros((2, grads_bias[0].shape[0]), full)
        ordered = lax.dynamic_update_index_in_dim(ordered, grads_bias[0], shard, 0)
        grad_in_bias = lax.dynamic_update_index_in_dim(ordered, grads_bias[1], 1 - shard, 0)
    else:
        grad_in_bias = grads_bias[0]
    sums = small_sum(
        jnp.concatenate(
            [
                jnp.stack(
                    [
                        grad_gain_one,
                        grad_shift_one,
                        jnp.sum(hidden_low.astype(full), axis=0),
                        grad_gain_two,
                        grad_shift_two,
                        jnp.sum(cot_float, axis=0),
                    ]
                ),
                grad_qv_bias,
                grad_in_bias.reshape(-1, width),
            ]
        ),
        ("shard", "heads", "tensor"),
    )
    owned = lax.dynamic_slice_in_dim(sums[:8], shard * shard_rows, shard_rows, 1)
    place = shard * depth + lax.axis_index("tensor")
    own_in_bias = lax.dynamic_slice_in_dim(
        sums[8:].reshape(-1), place * hidden_rows, hidden_rows, 0
    )
    return (
        output,
        input_grad,
        owned[0],
        owned[1],
        own_grad_qkv.astype(full),
        owned[6:8],
        own_out.astype(full),
        owned[2],
        owned[3],
        owned[4],
        own_in.astype(full),
        own_in_bias,
        own_back.astype(full),
        owned[5],
    )


def solution(mesh):
    in_specs = (
        P(("shard", "tensor"), "heads", None),
        P("shard"),
        P("shard"),
        P("shard", None),
        P(None, "shard"),
        P("shard", None),
        P("shard"),
        P("shard"),
        P("shard"),
        P(("shard", "tensor"), None),
        P(("shard", "tensor")),
        P(("shard", "tensor"), None),
        P("shard"),
        P(("shard", "tensor"), None),
        P(("shard", "tensor"), "heads", None),
    )
    out_specs = (
        P(("shard", "tensor"), "heads", None),
        P(("shard", "tensor"), "heads", None),
        P("shard"),
        P("shard"),
        P("shard", None),
        P(None, "shard"),
        P("shard", None),
        P("shard"),
        P("shard"),
        P("shard"),
        P(("shard", "tensor"), None),
        P(("shard", "tensor")),
        P(("shard", "tensor"), None),
        P("shard"),
    )
    return jax.shard_map(local, mesh=mesh, in_specs=in_specs, out_specs=out_specs, check_vma=False)
```
